32 devices in a mesh: blk: 16 (over z, x, core), rep: 2 (over y).
Axes of the slice: x: 2, y: 2, z: 4, core: 2. Of those that a mesh axis runs over, the one named last changes fastest.
Arguments:
- block_inputs: bfloat16 [5120, 4096], P(('blk', 'rep')), may hold values from -120 to 120
- out_cotangent: bfloat16 [5120, 4096], P(('blk', 'rep')), may hold values from -6 to 6
- dnormed_in: float32 [5120, 4096], P(('blk', 'rep')), may hold values from -6 to 6
- carried_sums: float32 [3, 1792, 4096], P(None, ('blk', 'rep')), may hold values from -128 to 128
- norm_gain: float32 [4096], replicated, may hold values from 0.1 to 1.9
- w_gate: bfloat16 [896, 4096], P('blk'), may hold values from -0.09375 to 0.09375
- w_up: bfloat16 [896, 4096], P('blk'), may hold values from -0.09375 to 0.09375
- w_down: bfloat16 [896, 4096], P('blk'), may hold values from -0.1875 to 0.1875
Outputs:
- input_grad: bfloat16 [5120, 4096], P(('blk', 'rep'))
- grad_gate: bfloat16 [896, 4096], P('blk')
- grad_up: bfloat16 [896, 4096], P('blk')
- grad_down: bfloat16 [896, 4096], P('blk')
The draws below stay inside these ranges and needn't reach their ends.
All inputs are finite; a program needn't handle non-finite values.
Results may differ from the reference program's by a relative error of at most 0.0038.
Values may be sent and summed in bfloat16 or wider, within the bound.
A program may use at most 64 MiB of HBM per device.

```python
import math
import jax
import jax.numpy as jnp
from jax import lax

D = 4096
FF_DEV = 56
CYCLE_STEPS = 6
GROUPS = 16
FF = 896
ROWS = 320
TOKENS = 5120
N_REP = 2


def draw_block_inputs(key, part):
    keys = jax.random.split(jax.random.fold_in(key, 17), 3)
    row_scale = jnp.exp(jax.random.uniform(keys[1], (TOKENS, 1), jnp.float32, 0.0, math.log(10.0)))
    col_scale = jnp.exp(jax.random.uniform(keys[2], (1, D), jnp.float32, math.log(0.3), math.log(3.0)))
    base = jax.random.normal(keys[0], (TOKENS, D), jnp.float32)
    base = jnp.clip(base, -4.0, 4.0)
    return jnp.clip(base * row_scale * col_scale, -120.0, 120.0).astype(jnp.bfloat16)


def levels(stream_key, extent, shards, low, top_value):
    gain = 1.0
    for position, shards_of in shards:
        heights = jax.random.uniform(jax.random.fold_in(jax.random.fold_in(stream_key, 6), position), (shards_of,), jnp.float32, low / len(shards), top_value / len(shards))
        gain = gain * jnp.repeat(jnp.exp(heights), extent[position] // shards_of).reshape((-1,) + (1,) * (len(extent) - 1 - position))
    return gain


def centred(own_key, shape, spread, reach, cuts=(), kind=jnp.bfloat16):
    gain = levels(own_key, shape, cuts, -0.22, 0.18) if cuts else 1.0
    values = jax.random.normal(own_key, shape, jnp.float32) * spread * gain
    return jnp.minimum(jnp.maximum(values, -reach), reach).astype(kind)


def setup_inputs(seed: int = 0) -> dict:
    key_list = jax.random.split(jax.random.key(seed), 9)
    return {
        "block_inputs": draw_block_inputs(jax.random.fold_in(key_list[8], 71), 0),
        "out_cotangent": centred(key_list[1], (TOKENS, D), 1.0, 6.0, ((0, 32),)),
        "dnormed_in": centred(key_list[2], (TOKENS, D), 1.0, 6.0, ((0, 32),), jnp.float32),
        "carried_sums": centred(key_list[3], (3, FF * N_REP, D), (0.3 * (GROUPS * ROWS) ** 0.5), 128.0, ((1, 32),), jnp.float32),
        "norm_gain": jnp.clip(1.0 + 0.18 * jax.random.normal(key_list[4], (D,), jnp.float32), 0.1, 1.9),
        "w_gate": centred(key_list[5], (FF, D), D ** -0.5, 0.09375, ((0, 16),)),
        "w_up": centred(key_list[6], (FF, D), D ** -0.5, 0.09375, ((0, 16),)),
        "w_down": centred(key_list[7], (FF, D), FF ** -0.5, 0.1875, ((0, 16),)),
    }


epsilon = 1e-05

def local_terms(normed, grad_in, gate_rows, up_rows, down_rows):
    gate = jnp.dot(normed, gate_rows.T, preferred_element_type=jnp.float32)
    upper = jnp.dot(normed, up_rows.T, preferred_element_type=jnp.float32)
    sigma = jax.nn.sigmoid(gate)
    act = gate * sigma
    hidden = (act * upper).astype(jnp.bfloat16)
    dhidden = jnp.dot(grad_in, down_rows.T, preferred_element_type=jnp.float32)
    dgate = (dhidden * upper * sigma * (1.0 + gate * (1.0 - sigma))).astype(jnp.bfloat16)
    dup = (dhidden * act).astype(jnp.bfloat16)
    dnormed = jnp.dot(dgate, gate_rows, preferred_element_type=jnp.float32) + jnp.dot(dup, up_rows, preferred_element_type=jnp.float32)
    terms = jnp.stack([jnp.dot(dgate.T, normed, preferred_element_type=jnp.float32), jnp.dot(dup.T, normed, preferred_element_type=jnp.float32), jnp.dot(hidden.T, grad_in, preferred_element_type=jnp.float32)])
    return (terms, dnormed)

def reference(block_inputs, out_cotangent, dnormed_in, carried_sums, norm_gain, w_gate, w_up, w_down):
    scale = 1.0 / math.sqrt(GROUPS * ROWS)
    inputs = block_inputs.reshape(GROUPS, ROWS, D)
    cotangents = out_cotangent.reshape(GROUPS, ROWS, D)
    partials = dnormed_in.reshape(GROUPS, ROWS, D)
    gates = w_gate.reshape(GROUPS, FF_DEV, D)
    uppers = w_up.reshape(GROUPS, FF_DEV, D)
    downs = w_down.reshape(GROUPS, FF_DEV, D)
    held = lax.optimization_barrier(jnp.sum(carried_sums.reshape(3, GROUPS, N_REP, FF_DEV, D), axis=2))
    start_totals = jnp.roll(held, CYCLE_STEPS, axis=1)

    def visit(totals, slot):
        grad_in = lax.dynamic_index_in_dim(cotangents, slot, 0, keepdims=False)
        carried = grad_in.astype(jnp.float32)
        values = lax.dynamic_index_in_dim(inputs, slot, 0, keepdims=False).astype(jnp.float32)
        rstd = lax.rsqrt(lax.optimization_barrier(jnp.mean(values * values, axis=-1, keepdims=True)) + epsilon)
        normed = (values * rstd * norm_gain).astype(jnp.bfloat16)
        dnormed = lax.dynamic_index_in_dim(partials, slot, 0, keepdims=False)
        for step in range(CYCLE_STEPS):
            group = ((slot + CYCLE_STEPS - step) % GROUPS).astype(jnp.int32)
            gate_rows = lax.dynamic_index_in_dim(gates, group, 0, keepdims=False)
            up_rows = lax.dynamic_index_in_dim(uppers, group, 0, keepdims=False)
            down_rows = lax.dynamic_index_in_dim(downs, group, 0, keepdims=False)
            terms, part = local_terms(normed, grad_in, gate_rows, up_rows, down_rows)
            dnormed = dnormed + part
            zero = jnp.int32(0)
            start = (zero, group, zero, zero)
            old = lax.dynamic_slice(totals, start, (3, 1, FF_DEV, D))
            totals = lax.dynamic_update_slice(totals, old + terms[:, None], start)
        scaled = norm_gain * dnormed
        dx = rstd * scaled - values * rstd ** 3 * lax.optimization_barrier(jnp.mean(values * scaled, axis=-1, keepdims=True))
        return (totals, (carried + dx).astype(jnp.bfloat16))
    totals, grads_in = lax.scan(visit, start_totals, jnp.arange(GROUPS, dtype=jnp.int32))
    rounded = (totals * scale).astype(jnp.bfloat16)
    grad_gate = rounded[0].reshape(FF, D)
    grad_up = rounded[1].reshape(FF, D)
    grad_down = rounded[2].reshape(FF, D)
    return (grads_in.reshape(TOKENS, D), grad_gate, grad_up, grad_down)
```

```python
import math

import jax
import jax.numpy as jnp
from jax import lax
from jax.sharding import PartitionSpec as P

CYCLE_STEPS = 6
CORES = 2
HOPS = CYCLE_STEPS // CORES

CHAIN = jnp.bfloat16
REP = jnp.bfloat16
SWAP = jnp.float32

epsilon = 1e-05


def moved(value, steps):
    count = lax.axis_size("blk")
    return lax.ppermute(value, "blk", [(i, (i + steps) % count) for i in range(count)])


def swapped_core(value):
    count = lax.axis_size("blk")
    return lax.ppermute(value, "blk", [(i, i ^ 1) for i in range(count)])


def swapped_rep(value):
    count = lax.axis_size("rep")
    return lax.ppermute(value, "rep", [(i, (i + 1) % count) for i in range(count)])


def swapped_rep_upper(value):
    reps = lax.axis_size("rep")
    pairs = [
        (i * reps + r, i * reps + (r + 1) % reps)
        for i in range(1, lax.axis_size("blk"), CORES)
        for r in range(reps)
    ]
    return lax.ppermute(value, ("blk", "rep"), pairs)


def group_terms(normed, grad_in, first, second, units):
    gu_rows = jnp.concatenate([first[: 2 * units], second[: 2 * units]], axis=0)
    down_rows = jnp.concatenate([first[2 * units :], second[2 * units :]], axis=0)
    gu = jnp.einsum("td,fd->tf", normed, gu_rows, preferred_element_type=jnp.float32)
    dhidden = jnp.einsum("td,fd->tf", grad_in, down_rows, preferred_element_type=jnp.float32)
    gu = gu.reshape(gu.shape[0], 2, 2, units)
    gate, upper = gu[:, :, 0], gu[:, :, 1]
    dhidden = dhidden.reshape(gate.shape)
    sigma = jax.nn.sigmoid(gate)
    act = gate * sigma
    hidden = (act * upper).astype(jnp.bfloat16).reshape(gate.shape[0], 2 * units)
    dgate = (dhidden * upper * sigma * (1.0 + gate * (1.0 - sigma))).astype(jnp.bfloat16)
    dup = (dhidden * act).astype(jnp.bfloat16)
    dgu = jnp.stack([dgate, dup], axis=2).reshape(gate.shape[0], 4 * units)
    dnormed = jnp.einsum("tf,fd->td", dgu, gu_rows, preferred_element_type=jnp.float32)
    t_gu = jnp.einsum("tf,td->fd", dgu, normed, preferred_element_type=jnp.float32)
    t_down = jnp.einsum("tf,td->fd", hidden, grad_in, preferred_element_type=jnp.float32)
    own = jnp.concatenate([t_gu[: 2 * units], t_down[:units]], axis=0)
    other = jnp.concatenate([t_gu[2 * units :], t_down[units:]], axis=0)
    return own, other, dnormed


def shards(block_inputs, out_cotangent, dnormed_in, carried_sums, norm_gain, w_gate, w_up, w_down):
    reps = lax.axis_size("rep")
    scale = 1.0 / math.sqrt(lax.axis_size("blk") * block_inputs.shape[0] * reps)
    core = lax.rem(lax.axis_index("blk"), CORES)
    rep = lax.axis_index("rep")
    units, width = w_gate.shape
    half = width // 2

    def mine(v):
        return lax.dynamic_slice_in_dim(v, rep * half, half, axis=v.ndim - 1)

    def theirs(v):
        return lax.dynamic_slice_in_dim(v, (1 - rep) * half, half, axis=v.ndim - 1)

    def joined(a, b):
        return jnp.where(rep == 0, jnp.concatenate([a, b], -1), jnp.concatenate([b, a], -1))

    def summed(v):
        return mine(v) + swapped_rep(theirs(v).astype(REP)).astype(jnp.float32)

    own_weights = jnp.concatenate([w_gate, w_up, w_down], axis=0)
    piece = mine(own_weights)
    fulls = []
    for _ in range(HOPS):
        piece = moved(piece, -CORES)
        fulls.append(joined(piece, swapped_rep(piece)))

    carried = carried_sums.reshape(3 * units, width)
    held = None
    if CHAIN != jnp.float32:
        held = mine(carried) + swapped_rep(theirs(carried))
        held = moved(held, CYCLE_STEPS)

    values = block_inputs.astype(jnp.float32)
    rstd = lax.rsqrt(jnp.mean(values * values, axis=-1, keepdims=True) + epsilon)
    normed = (values * rstd * norm_gain).astype(jnp.bfloat16)

    dnormed = dnormed_in
    reduced = []
    for j in range(HOPS):
        if j < HOPS - 1:
            other = swapped_core(fulls[j])
        else:
            other = swapped_core(jnp.where(core == 0, fulls[j], own_weights))
        own_term, other_term, part = group_terms(normed, out_cotangent, fulls[j], other, units)
        dnormed = dnormed + part
        received = swapped_core(other_term.astype(SWAP)).astype(jnp.float32)
        if j < HOPS - 1:
            reduced.append(own_term + received)
        else:
            last = own_term + jnp.where(core == 0, received, 0.0)
            if held is None:
                last = last + carried
            reduced.append(last)
            near = mine(received) + swapped_rep_upper(theirs(received).astype(REP)).astype(
                jnp.float32
            )
            near = jnp.where(core == 0, 0.0, near)

    sums = summed(reduced[HOPS - 1])
    for j in range(HOPS - 2, -1, -1):
        sums = moved(sums.astype(CHAIN), CORES).astype(jnp.float32) + summed(reduced[j])
    sums = moved(sums.astype(CHAIN), CORES).astype(jnp.float32) + near
    if held is not None:
        sums = sums + held
    rounded = (sums * scale).astype(jnp.bfloat16)
    finals = joined(rounded, swapped_rep(rounded))

    scaled = norm_gain * dnormed
    dx = rstd * scaled - values * rstd**3 * jnp.mean(values * scaled, axis=-1, keepdims=True)
    input_grad = (out_cotangent.astype(jnp.float32) + dx).astype(jnp.bfloat16)
    return (input_grad, finals[:units], finals[units : 2 * units], finals[2 * units :])


def solution(mesh):
    placed = (
        P(("blk", "rep"), None),
        P(("blk", "rep"), None),
        P(("blk", "rep"), None),
        P(None, ("blk", "rep"), None),
        P(),
        P("blk", None),
        P("blk", None),
        P("blk", None),
    )
    return jax.shard_map(
        shards,
        mesh=mesh,
        in_specs=placed,
        out_specs=(P(("blk", "rep"), None), P("blk", None), P("blk", None), P("blk", None)),
        check_vma=False,
    )
```

```python
import math

import jax
import jax.numpy as jnp
from jax import lax
from jax.experimental import pallas as pl
from jax.experimental.pallas import tpu as pltpu
from jax.sharding import PartitionSpec as P

CYCLE_STEPS = 6
CORES = 2
HOPS = CYCLE_STEPS // CORES

CHAIN = jnp.bfloat16
REP = jnp.bfloat16
SWAP = jnp.float32

epsilon = 1e-05
SPLIT = 2
ROWS16 = 16
MESH = pl.DeviceIdType.MESH


def moved(value, steps):
    count = lax.axis_size("blk")
    return lax.ppermute(value, "blk", [(i, (i + steps) % count) for i in range(count)])


def swapped_core(value):
    count = lax.axis_size("blk")
    return lax.ppermute(value, "blk", [(i, i ^ 1) for i in range(count)])


def swapped_rep(value):
    count = lax.axis_size("rep")
    return lax.ppermute(value, "rep", [(i, (i + 1) % count) for i in range(count)])


def swapped_rep_upper(value):
    reps = lax.axis_size("rep")
    pairs = [
        (i * reps + r, i * reps + (r + 1) % reps)
        for i in range(1, lax.axis_size("blk"), CORES)
        for r in range(reps)
    ]
    return lax.ppermute(value, ("blk", "rep"), pairs)


def gather_kernel(
    chips, w_ref, mine_ref, theirs_ref, out_ref, held_ref, home_buf, twin_buf,
    ring_send, ring_recv, rep_send, rep_recv, core_send, core_recv, swap_sem, home_sem,
):
    blk = lax.axis_index("blk")
    rep = lax.axis_index("rep")
    core = lax.rem(blk, CORES)
    count = chips * CORES
    odd = lax.rem(blk // CORES, 2)
    before = (lax.rem(blk + count - 2 * CORES, count), rep)
    after = (lax.rem(blk + 2 * CORES, count), rep)
    beside = (blk + CORES * (1 - 2 * odd), rep)
    sibling = (blk + 1 - 2 * core, rep)
    twin = (blk, 1 - rep)
    ahead = (lax.rem(blk + CYCLE_STEPS, count), rep)
    behind = (lax.rem(blk + count - CYCLE_STEPS, count), rep)
    part = w_ref.shape[1] // (2 * SPLIT)

    barrier = pltpu.get_barrier_semaphore()
    for peer in (before, after, beside, sibling, twin, ahead, behind):
        pl.semaphore_signal(barrier, inc=1, device_id=peer, device_id_type=MESH)
    pl.semaphore_wait(barrier, 7)

    def lanes(owner, s):
        return pl.ds(pl.multiple_of((owner * SPLIT + s) * part, part), part)

    def ring(j, s, src, target, out=None):
        return pltpu.make_async_remote_copy(
            src_ref=src.at[:, lanes(rep, s)],
            dst_ref=out_ref.at[2 * j].at[:, lanes(rep, s)],
            send_sem=ring_send.at[j if out is None else out, s],
            recv_sem=ring_recv.at[j, s],
            device_id=target,
            device_id_type=MESH,
        )

    def to_twin(j, s, owner):
        return pltpu.make_async_remote_copy(
            src_ref=out_ref.at[2 * j].at[:, lanes(owner, s)],
            dst_ref=out_ref.at[2 * j].at[:, lanes(owner, s)],
            send_sem=rep_send.at[j, s],
            recv_sem=rep_recv.at[j, s],
            device_id=twin,
            device_id_type=MESH,
        )

    def to_sibling(j, s, owner, side, src):
        return pltpu.make_async_remote_copy(
            src_ref=src.at[:, lanes(owner, s)],
            dst_ref=out_ref.at[2 * j + 1].at[:, lanes(owner, s)],
            send_sem=core_send.at[j, s, side],
            recv_sem=core_recv.at[j, s, side],
            device_id=sibling,
            device_id_type=MESH,
        )

    last = HOPS - 1

    def pass_to_sibling(j, s, owner, side):
        if j < last:
            to_sibling(j, s, owner, side, out_ref.at[2 * j]).start()
        else:
            @pl.when(core == 0)
            def _():
                to_sibling(j, s, owner, side, out_ref.at[2 * j]).start()

    swap = pltpu.make_async_remote_copy(
        src_ref=theirs_ref,
        dst_ref=twin_buf,
        send_sem=swap_sem.at[0],
        recv_sem=swap_sem.at[1],
        device_id=twin,
        device_id_type=MESH,
    )
    home = pltpu.make_async_remote_copy(
        src_ref=home_buf,
        dst_ref=held_ref,
        send_sem=home_sem.at[0],
        recv_sem=home_sem.at[1],
        device_id=ahead,
        device_id_type=MESH,
    )
    swap.start()
    for s in range(SPLIT):
        ring(1, s, w_ref, before).start()

    @pl.when(odd == 1)
    def _():
        for s in range(SPLIT):
            ring(0, s, w_ref, beside).start()

    @pl.when(core == 1)
    def _():
        for s in range(SPLIT):
            for side, owner in enumerate((rep, 1 - rep)):
                to_sibling(last, s, owner, side, w_ref).start()

    def on_ring(j):
        for s in range(SPLIT):
            ring(j, s, w_ref, before).wait_recv()
            if j == 1:
                @pl.when(odd == 1)
                def _():
                    ring(2, s, out_ref.at[2], beside).start()

                @pl.when(odd == 0)
                def _():
                    ring(0, s, out_ref.at[2], beside).start()
            if j == 0:
                @pl.when(odd == 1)
                def _():
                    ring(2, s, out_ref.at[0], before, HOPS).start()
            to_twin(j, s, rep).start()
            pass_to_sibling(j, s, rep, 0)

    def on_twin(j):
        for s in range(SPLIT):
            to_twin(j, s, 1 - rep).wait_recv()
            pass_to_sibling(j, s, 1 - rep, 1)

    on_ring(1)
    swap.wait()

    def add(i, _):
        at = pl.ds(pl.multiple_of(i * ROWS16, ROWS16), ROWS16)
        total = mine_ref[at, :] + twin_buf[at, :].astype(jnp.float32)
        home_buf[at, :] = total.astype(home_buf.dtype)
        return _

    lax.fori_loop(0, mine_ref.shape[0] // ROWS16, add, 0)
    home.start()
    on_ring(0)
    on_twin(1)
    on_ring(2)
    on_twin(0)
    on_twin(2)
    for j in range(HOPS):
        for s in range(SPLIT):
            if j < 2:
                ring(j, s, w_ref, before).wait_send()
            to_twin(j, s, rep).wait_send()
            for side, owner in enumerate((rep, 1 - rep)):
                copy = to_sibling(j, s, owner, side, w_ref)
                copy.wait_send()
                copy.wait_recv()
    home.wait()

    @pl.when(odd == 1)
    def _():
        for s in range(SPLIT):
            ring(2, s, w_ref, beside).wait_send()
            ring(2, s, w_ref, before, HOPS).wait_send()


def gathered(own_weights, mine, theirs):
    rows, width = own_weights.shape
    chips = lax.axis_size("blk") // CORES
    return pl.pallas_call(
        lambda *refs: gather_kernel(chips, *refs),
        out_shape=(
            jax.ShapeDtypeStruct((2 * HOPS, rows, width), own_weights.dtype),
            jax.ShapeDtypeStruct(theirs.shape, theirs.dtype),
        ),
        in_specs=[
            pl.BlockSpec(memory_space=pl.ANY),
            pl.BlockSpec(memory_space=pltpu.VMEM),
            pl.BlockSpec(memory_space=pl.ANY),
        ],
        out_specs=(pl.BlockSpec(memory_space=pl.ANY),) * 2,
        scratch_shapes=[
            pltpu.VMEM(mine.shape, theirs.dtype),
            pltpu.VMEM(mine.shape, theirs.dtype),
            pltpu.SemaphoreType.DMA((HOPS + 1, SPLIT)),
            pltpu.SemaphoreType.DMA((HOPS, SPLIT)),
            pltpu.SemaphoreType.DMA((HOPS, SPLIT)),
            pltpu.SemaphoreType.DMA((HOPS, SPLIT)),
            pltpu.SemaphoreType.DMA((HOPS, SPLIT, 2)),
            pltpu.SemaphoreType.DMA((HOPS, SPLIT, 2)),
            pltpu.SemaphoreType.DMA((2,)),
            pltpu.SemaphoreType.DMA((2,)),
        ],
        compiler_params=pltpu.CompilerParams(
            collective_id=0, has_side_effects=True, vmem_limit_bytes=16 * 2**20
        ),
        name="gather_weights",
    )(own_weights, mine, theirs)


def group_terms(normed, grad_in, groups, units):
    tokens, width = normed.shape
    count, rows, _ = groups.shape
    flat = groups.reshape(count * rows, width)
    left = jnp.einsum("td,fd->tf", normed, flat, preferred_element_type=jnp.float32)
    right = jnp.einsum("td,fd->tf", grad_in, flat, preferred_element_type=jnp.float32)
    left = left.reshape(tokens, count, rows)
    gate, upper = left[:, :, :units], left[:, :, units : 2 * units]
    dhidden = right.reshape(tokens, count, rows)[:, :, 2 * units : 3 * units]
    sigma = jax.nn.sigmoid(gate)
    act = gate * sigma
    hidden = (act * upper).astype(jnp.bfloat16)
    dgate = (dhidden * upper * sigma * (1.0 + gate * (1.0 - sigma))).astype(jnp.bfloat16)
    dup = (dhidden * act).astype(jnp.bfloat16)
    rest = rows - 2 * units
    dgu = jnp.pad(jnp.concatenate([dgate, dup], axis=2), ((0, 0), (0, 0), (0, rest)))
    dgu = dgu.reshape(tokens, count * rows)
    hid = jnp.pad(hidden, ((0, 0), (0, 0), (2 * units, rest - units)))
    hid = hid.reshape(tokens, count * rows)
    dnormed = jnp.einsum("tf,fd->td", dgu, flat, preferred_element_type=jnp.float32)
    terms = jnp.einsum(
        "tf,td->fd",
        jnp.concatenate([dgu, hid], axis=0),
        jnp.concatenate([normed, grad_in], axis=0),
        preferred_element_type=jnp.float32,
    )
    return terms.reshape(count, rows, width), dnormed


def shards(block_inputs, out_cotangent, dnormed_in, carried_sums, norm_gain, w_gate, w_up, w_down):
    reps = lax.axis_size("rep")
    scale = 1.0 / math.sqrt(lax.axis_size("blk") * block_inputs.shape[0] * reps)
    core = lax.rem(lax.axis_index("blk"), CORES)
    rep = lax.axis_index("rep")
    units, width = w_gate.shape
    half = width // 2

    def mine(v):
        return lax.dynamic_slice_in_dim(v, rep * half, half, axis=v.ndim - 1)

    def theirs(v):
        return lax.dynamic_slice_in_dim(v, (1 - rep) * half, half, axis=v.ndim - 1)

    def joined(a, b):
        return jnp.where(rep == 0, jnp.concatenate([a, b], -1), jnp.concatenate([b, a], -1))

    def summed(v):
        return mine(v) + swapped_rep(theirs(v).astype(REP)).astype(jnp.float32)

    spare = jnp.zeros((-3 * units % ROWS16, width), w_gate.dtype)
    carried = jnp.pad(carried_sums.reshape(3 * units, width), ((0, spare.shape[0]), (0, 0)))
    groups, held = gathered(
        jnp.concatenate([w_gate, w_up, w_down, spare], axis=0),
        mine(carried),
        theirs(carried).astype(REP),
    )
    held = held[: 3 * units].astype(jnp.float32)

    values = block_inputs.astype(jnp.float32)
    rstd = lax.rsqrt(jnp.mean(values * values, axis=-1, keepdims=True) + epsilon)
    normed = (values * rstd * norm_gain).astype(jnp.bfloat16)

    terms, part = group_terms(normed, out_cotangent, groups, units)
    terms = terms[:, : 3 * units]
    dnormed = dnormed_in + part
    reduced = []
    for j in range(HOPS):
        own_term, other_term = terms[2 * j], terms[2 * j + 1]
        received = swapped_core(other_term.astype(SWAP)).astype(jnp.float32)
        if j < HOPS - 1:
            reduced.append(own_term + received)
        else:
            last = own_term + jnp.where(core == 0, received, 0.0)
            reduced.append(last)
            near = mine(received) + swapped_rep_upper(theirs(received).astype(REP)).astype(
                jnp.float32
            )
            near = jnp.where(core == 0, 0.0, near)

    sums = summed(reduced[HOPS - 1])
    for j in range(HOPS - 2, -1, -1):
        sums = moved(sums.astype(CHAIN), CORES).astype(jnp.float32) + summed(reduced[j])
    sums = moved(sums.astype(CHAIN), CORES).astype(jnp.float32) + near
    rounded = ((sums + held) * scale).astype(jnp.bfloat16)
    finals = joined(rounded, swapped_rep(rounded))

    scaled = norm_gain * dnormed
    dx = rstd * scaled - values * rstd**3 * jnp.mean(values * scaled, axis=-1, keepdims=True)
    input_grad = (out_cotangent.astype(jnp.float32) + dx).astype(jnp.bfloat16)
    return (input_grad, finals[:units], finals[units : 2 * units], finals[2 * units :])


def solution(mesh):
    placed = (
        P(("blk", "rep"), None),
        P(("blk", "rep"), None),
        P(("blk", "rep"), None),
        P(None, ("blk", "rep"), None),
        P(),
        P("blk", None),
        P("blk", None),
        P("blk", None),
    )
    return jax.shard_map(
        shards,
        mesh=mesh,
        in_specs=placed,
        out_specs=(P(("blk", "rep"), None), P("blk", None), P("blk", None), P("blk", None)),
        check_vma=False,
    )
```

```python
import math

import jax
import jax.numpy as jnp
from jax import lax
from jax.experimental import pallas as pl
from jax.experimental.pallas import tpu as pltpu
from jax.sharding import PartitionSpec as P

CYCLE_STEPS = 6
CORES = 2
HOPS = CYCLE_STEPS // CORES

CHAIN = jnp.bfloat16
REP = jnp.bfloat16
SWAP = jnp.float32

epsilon = 1e-05
SPLIT = 2
ROWS16 = 16
MESH = pl.DeviceIdType.MESH


def moved(value, steps):
    count = lax.axis_size("blk")
    return lax.ppermute(value, "blk", [(i, (i + steps) % count) for i in range(count)])


def swapped_core(value):
    count = lax.axis_size("blk")
    return lax.ppermute(value, "blk", [(i, i ^ 1) for i in range(count)])


def swapped_rep(value):
    count = lax.axis_size("rep")
    return lax.ppermute(value, "rep", [(i, (i + 1) % count) for i in range(count)])


def swapped_rep_upper(value):
    reps = lax.axis_size("rep")
    pairs = [
        (i * reps + r, i * reps + (r + 1) % reps)
        for i in range(1, lax.axis_size("blk"), CORES)
        for r in range(reps)
    ]
    return lax.ppermute(value, ("blk", "rep"), pairs)


def gather_kernel(
    chips, w_ref, mine_ref, theirs_ref, out_ref, held_ref, home_buf, twin_buf,
    ring_send, ring_recv, rep_send, rep_recv, core_send, core_recv, swap_sem, home_sem,
):
    blk = lax.axis_index("blk")
    rep = lax.axis_index("rep")
    core = lax.rem(blk, CORES)
    count = chips * CORES
    odd = lax.rem(blk // CORES, 2)
    before = (lax.rem(blk + count - 2 * CORES, count), rep)
    after = (lax.rem(blk + 2 * CORES, count), rep)
    beside = (blk + CORES * (1 - 2 * odd), rep)
    sibling = (blk + 1 - 2 * core, rep)
    twin = (blk, 1 - rep)
    ahead = (lax.rem(blk + CYCLE_STEPS, count), rep)
    behind = (lax.rem(blk + count - CYCLE_STEPS, count), rep)
    part = w_ref.shape[1] // (2 * SPLIT)

    barrier = pltpu.get_barrier_semaphore()
    for peer in (before, after, beside, sibling, twin, ahead, behind):
        pl.semaphore_signal(barrier, inc=1, device_id=peer, device_id_type=MESH)
    pl.semaphore_wait(barrier, 7)

    def lanes(owner, s):
        return pl.ds(pl.multiple_of((owner * SPLIT + s) * part, part), part)

    def ring(j, s, src, target, out=None):
        return pltpu.make_async_remote_copy(
            src_ref=src.at[:, lanes(rep, s)],
            dst_ref=out_ref.at[2 * j].at[:, lanes(rep, s)],
            send_sem=ring_send.at[j if out is None else out, s],
            recv_sem=ring_recv.at[j, s],
            device_id=target,
            device_id_type=MESH,
        )

    def to_twin(j, s, owner):
        return pltpu.make_async_remote_copy(
            src_ref=out_ref.at[2 * j].at[:, lanes(owner, s)],
            dst_ref=out_ref.at[2 * j].at[:, lanes(owner, s)],
            send_sem=rep_send.at[j, s],
            recv_sem=rep_recv.at[j, s],
            device_id=twin,
            device_id_type=MESH,
        )

    def to_sibling(j, s, owner, side, src):
        return pltpu.make_async_remote_copy(
            src_ref=src.at[:, lanes(owner, s)],
            dst_ref=out_ref.at[2 * j + 1].at[:, lanes(owner, s)],
            send_sem=core_send.at[j, s, side],
            recv_sem=core_recv.at[j, s, side],
            device_id=sibling,
            device_id_type=MESH,
        )

    last = HOPS - 1

    def pass_to_sibling(j, s, owner, side):
        if j < last:
            to_sibling(j, s, owner, side, out_ref.at[2 * j]).start()
        else:
            @pl.when(core == 0)
            def _():
                to_sibling(j, s, owner, side, out_ref.at[2 * j]).start()

    swap = pltpu.make_async_remote_copy(
        src_ref=theirs_ref,
        dst_ref=twin_buf,
        send_sem=swap_sem.at[0],
        recv_sem=swap_sem.at[1],
        device_id=twin,
        device_id_type=MESH,
    )
    home = pltpu.make_async_remote_copy(
        src_ref=home_buf,
        dst_ref=held_ref,
        send_sem=home_sem.at[0],
        recv_sem=home_sem.at[1],
        device_id=ahead,
        device_id_type=MESH,
    )
    swap.start()
    for s in range(SPLIT):
        ring(1, s, w_ref, before).start()

    @pl.when(odd == 1)
    def _():
        for s in range(SPLIT):
            ring(0, s, w_ref, beside).start()

    @pl.when(core == 1)
    def _():
        for s in range(SPLIT):
            for side, owner in enumerate((rep, 1 - rep)):
                to_sibling(last, s, owner, side, w_ref).start()

    def on_ring(j):
        for s in range(SPLIT):
            ring(j, s, w_ref, before).wait_recv()
            if j == 1:
                @pl.when(odd == 1)
                def _():
                    ring(2, s, out_ref.at[2], beside).start()

                @pl.when(odd == 0)
                def _():
                    ring(0, s, out_ref.at[2], beside).start()
            if j == 0:
                @pl.when(odd == 1)
                def _():
                    ring(2, s, out_ref.at[0], before, HOPS).start()
            to_twin(j, s, rep).start()
            pass_to_sibling(j, s, rep, 0)

    def on_twin(j):
        for s in range(SPLIT):
            to_twin(j, s, 1 - rep).wait_recv()
            pass_to_sibling(j, s, 1 - rep, 1)

    on_ring(1)
    swap.wait()

    def add(i, _):
        at = pl.ds(pl.multiple_of(i * ROWS16, ROWS16), ROWS16)
        total = mine_ref[at, :] + twin_buf[at, :].astype(jnp.float32)
        home_buf[at, :] = total.astype(home_buf.dtype)
        return _

    lax.fori_loop(0, mine_ref.shape[0] // ROWS16, add, 0)
    home.start()
    on_ring(0)
    on_twin(1)
    on_ring(2)
    on_twin(0)
    on_twin(2)
    for j in range(HOPS):
        for s in range(SPLIT):
            if j < 2:
                ring(j, s, w_ref, before).wait_send()
            to_twin(j, s, rep).wait_send()
            for side, owner in enumerate((rep, 1 - rep)):
                copy = to_sibling(j, s, owner, side, w_ref)
                copy.wait_send()
                copy.wait_recv()
    home.wait()

    @pl.when(odd == 1)
    def _():
        for s in range(SPLIT):
            ring(2, s, w_ref, beside).wait_send()
            ring(2, s, w_ref, before, HOPS).wait_send()


def gathered(own_weights, mine, theirs):
    rows, width = own_weights.shape
    chips = lax.axis_size("blk") // CORES
    return pl.pallas_call(
        lambda *refs: gather_kernel(chips, *refs),
        out_shape=(
            jax.ShapeDtypeStruct((2 * HOPS, rows, width), own_weights.dtype),
            jax.ShapeDtypeStruct(theirs.shape, theirs.dtype),
        ),
        in_specs=[
            pl.BlockSpec(memory_space=pl.ANY),
            pl.BlockSpec(memory_space=pltpu.VMEM),
            pl.BlockSpec(memory_space=pl.ANY),
        ],
        out_specs=(pl.BlockSpec(memory_space=pl.ANY),) * 2,
        scratch_shapes=[
            pltpu.VMEM(mine.shape, theirs.dtype),
            pltpu.VMEM(mine.shape, theirs.dtype),
            pltpu.SemaphoreType.DMA((HOPS + 1, SPLIT)),
            pltpu.SemaphoreType.DMA((HOPS, SPLIT)),
            pltpu.SemaphoreType.DMA((HOPS, SPLIT)),
            pltpu.SemaphoreType.DMA((HOPS, SPLIT)),
            pltpu.SemaphoreType.DMA((HOPS, SPLIT, 2)),
            pltpu.SemaphoreType.DMA((HOPS, SPLIT, 2)),
            pltpu.SemaphoreType.DMA((2,)),
            pltpu.SemaphoreType.DMA((2,)),
        ],
        compiler_params=pltpu.CompilerParams(
            collective_id=0, has_side_effects=True, vmem_limit_bytes=16 * 2**20
        ),
        name="gather_weights",
    )(own_weights, mine, theirs)


def group_terms(normed, grad_in, groups, units):
    tokens, width = normed.shape
    count, rows, _ = groups.shape
    flat = groups.reshape(count * rows, width)
    left = jnp.einsum("td,fd->tf", normed, flat, preferred_element_type=jnp.float32)
    right = jnp.einsum("td,fd->tf", grad_in, flat, preferred_element_type=jnp.float32)
    lane = lax.broadcasted_iota(jnp.int32, (1, count * rows), 1)
    used = lax.rem(lane, rows) < units
    gate, upper = left, jnp.roll(left, -units, axis=1)
    dhidden = jnp.roll(right, -2 * units, axis=1)
    sigma = jax.nn.sigmoid(gate)
    act = gate * sigma
    hidden = jnp.where(used, act * upper, 0.0).astype(jnp.bfloat16)
    dgate = dhidden * upper * sigma * (1.0 + gate * (1.0 - sigma))
    dgate = jnp.where(used, dgate, 0.0).astype(jnp.bfloat16)
    dup = jnp.where(used, dhidden * act, 0.0).astype(jnp.bfloat16)
    dgu = dgate + jnp.roll(dup, units, axis=1)
    hid = jnp.roll(hidden, 2 * units, axis=1)
    dnormed = jnp.einsum("tf,fd->td", dgu, flat, preferred_element_type=jnp.float32)
    terms = jnp.einsum(
        "tf,td->fd",
        jnp.concatenate([dgu, hid], axis=0),
        jnp.concatenate([normed, grad_in], axis=0),
        preferred_element_type=jnp.float32,
    )
    return terms.reshape(count, rows, width), dnormed


def shards(block_inputs, out_cotangent, dnormed_in, carried_sums, norm_gain, w_gate, w_up, w_down):
    reps = lax.axis_size("rep")
    scale = 1.0 / math.sqrt(lax.axis_size("blk") * block_inputs.shape[0] * reps)
    core = lax.rem(lax.axis_index("blk"), CORES)
    rep = lax.axis_index("rep")
    units, width = w_gate.shape
    half = width // 2

    def mine(v):
        return lax.dynamic_slice_in_dim(v, rep * half, half, axis=v.ndim - 1)

    def theirs(v):
        return lax.dynamic_slice_in_dim(v, (1 - rep) * half, half, axis=v.ndim - 1)

    def joined(a, b):
        return jnp.where(rep == 0, jnp.concatenate([a, b], -1), jnp.concatenate([b, a], -1))

    def summed(v):
        return mine(v) + swapped_rep(theirs(v).astype(REP)).astype(jnp.float32)

    spare = jnp.zeros((-3 * units % ROWS16, width), w_gate.dtype)
    carried = jnp.pad(carried_sums.reshape(3 * units, width), ((0, spare.shape[0]), (0, 0)))
    groups, held = gathered(
        jnp.concatenate([w_gate, w_up, w_down, spare], axis=0),
        mine(carried),
        theirs(carried).astype(REP),
    )
    held = held[: 3 * units].astype(jnp.float32)

    values = block_inputs.astype(jnp.float32)
    rstd = lax.rsqrt(jnp.mean(values * values, axis=-1, keepdims=True) + epsilon)
    normed = (values * rstd * norm_gain).astype(jnp.bfloat16)

    terms, part = group_terms(normed, out_cotangent, groups, units)
    terms = terms[:, : 3 * units]
    dnormed = dnormed_in + part
    reduced = []
    for j in range(HOPS):
        own_term, other_term = terms[2 * j], terms[2 * j + 1]
        received = swapped_core(other_term.astype(SWAP)).astype(jnp.float32)
        if j < HOPS - 1:
            reduced.append(own_term + received)
        else:
            last = own_term + jnp.where(core == 0, received, 0.0)
            reduced.append(last)
            near = mine(received) + swapped_rep_upper(theirs(received).astype(REP)).astype(
                jnp.float32
            )
            near = jnp.where(core == 0, 0.0, near)

    sums = summed(reduced[HOPS - 1])
    for j in range(HOPS - 2, -1, -1):
        sums = moved(sums.astype(CHAIN), CORES).astype(jnp.float32) + summed(reduced[j])
    sums = moved(sums.astype(CHAIN), CORES).astype(jnp.float32) + near
    rounded = ((sums + held) * scale).astype(jnp.bfloat16)
    finals = joined(rounded, swapped_rep(rounded))

    scaled = norm_gain * dnormed
    dx = rstd * scaled - values * rstd**3 * jnp.mean(values * scaled, axis=-1, keepdims=True)
    input_grad = (out_cotangent.astype(jnp.float32) + dx).astype(jnp.bfloat16)
    return (input_grad, finals[:units], finals[units : 2 * units], finals[2 * units :])


def solution(mesh):
    placed = (
        P(("blk", "rep"), None),
        P(("blk", "rep"), None),
        P(("blk", "rep"), None),
        P(None, ("blk", "rep"), None),
        P(),
        P("blk", None),
        P("blk", None),
        P("blk", None),
    )
    return jax.shard_map(
        shards,
        mesh=mesh,
        in_specs=placed,
        out_specs=(P(("blk", "rep"), None), P("blk", None), P("blk", None), P("blk", None)),
        check_vma=False,
    )
```
